32 devices in a mesh: groups: 2 (over y), dp: 4 (over z), mp: 4 (over x, core).
Axes of the slice: x: 2, y: 2, z: 4, core: 2. Of those that a mesh axis runs over, the one named last changes fastest.
Arguments:
- replay: bfloat16 [8192, 1024], P(('groups', 'dp'), 'mp'), parts along dimension 0, may hold values from -17 to 17
- sa_row: int32 [1024], P(('groups', 'dp')), parts along dimension 0, may hold values from 0 to 1023
- goal_owner: int32 [1024, 1], P(('groups', 'dp')), parts along dimension 0, may hold values from 0 to 3; in each aligned block of 128 rows (0 to 127, 128 to 255, ...) at most 64 rows name the same one
- goal_row: int32 [1024], P(('groups', 'dp')), parts along dimension 0, may hold values from 0 to 1023
- state_first: bfloat16 [1024, 2048], P(None, 'mp'), may hold values from -0.1875 to 0.1875
- state_second: bfloat16 [2048, 1024], P('mp'), may hold values from -0.125 to 0.125
- goal_first: bfloat16 [1024, 2048], P(None, 'mp'), may hold values from -0.1875 to 0.1875
- goal_second: bfloat16 [2048, 1024], P('mp'), may hold values from -0.125 to 0.125
Outputs:
- state_first_grad: float32 [2048, 2048], P(('groups', 'dp'), 'mp'), parts along dimension 0
- state_second_grad: float32 [4096, 1024], P(('groups', 'mp'), 'dp'), parts along dimension 0
- goal_first_grad: float32 [2048, 2048], P(('groups', 'dp'), 'mp'), parts along dimension 0
- goal_second_grad: float32 [4096, 1024], P(('groups', 'mp'), 'dp'), parts along dimension 0
The draws below stay inside these ranges and needn't reach their ends.
There are 2 independent parts, one for each index of `groups`. The reference program is written for one: setup_inputs(seed, part) draws one part's arguments, and reference() takes and returns one part's arrays. A program takes and returns all parts, laid end to end along the dimension named above; an argument that names none is the same for every part. Nothing has to cross between parts.
Inputs may be any that keep to these rules, and one draw needn't show every extreme that they name: `goal_owner`: within the 128 rows of one device no owner is named more than 64 times, and in every draw some owner is named exactly 64 times by the rows of some device.
All inputs are finite; a program needn't handle non-finite values.
Results may differ from the reference program's by a relative error of at most 0.01615.
Values may be sent and summed in bfloat16 or wider, within the bound.
No kernel may reach another device: no remote copies, remote signals or barrier semaphores. Data moves between devices by JAX's collectives and lax.ppermute only.
A program may use at most 64 MiB of HBM per device.

```python
import math
import jax
import jax.numpy as jnp
import numpy as np
from jax import lax

LATENT = 1024
UNITS = 2048
EMBED = 1024
ROWS_DEV = 128
REPLAY_DEV = 1024
BATCH = 512
REPLAY = 4096
CAP = 64
N_DP = 4


def draw_replay(key, part):
    key = jax.random.fold_in(key, 11)
    noise_key = jax.random.fold_in(key, 0)
    return jax.random.truncated_normal(noise_key, -6.0, 6.0, (REPLAY, LATENT), jnp.float32).astype(jnp.bfloat16)


def touch_ends(values, stream_key, least, high):
    longest = values.shape.index(max(values.shape))
    spots = []
    for shift in (0, 1):
        where = [jax.random.randint(jax.random.fold_in(stream_key, axis), (), 0, length) for axis, length in enumerate(values.shape)]
        where[longest] = (where[longest] + shift) % values.shape[longest]
        spots.append(tuple(where))
    return values.at[spots[0]].set(least).at[spots[1]].set(high)


def block_scale(key, extent, shards, smallest, top_value):
    factor_of, own = 1.0, jax.random.fold_in(key, 6)
    for axis_at, blocks in shards:
        steps = jnp.exp(jax.random.uniform(jax.random.fold_in(own, axis_at), (blocks,), jnp.float32, smallest / len(shards), top_value / len(shards)))
        factor_of = factor_of * jnp.repeat(steps, extent[axis_at] // blocks).reshape([-1 if axis == axis_at else 1 for axis in range(len(extent))])
    return factor_of


def routed_block(key, own, number, rows, amount, top, bound, skew):
    sequence = jax.random.permutation(key, amount)
    packed, usual = portions_of(amount, rows * top, bound, skew, True), portions_of(amount, rows * top, bound, skew, False)
    places = jnp.arange(amount)

    def named(tallies, offset_by):
        used = int((tallies > 0).sum())
        fixed = max(1, used // 4)
        shifted = fixed + (places - fixed + offset_by * (used - fixed)) % max(1, amount - fixed)
        return jnp.zeros((amount,), jnp.int32).at[sequence[jnp.where(places < fixed, places, shifted)]].set(jnp.asarray(tallies, jnp.int32))

    tallies = jnp.where(number % 4 == 0, named(packed, number // 4), named(usual, number - number // 4 - 1))
    mixed = jax.random.permutation(jax.random.fold_in(own, 3), amount)
    giver, receiver = mixed[0:amount // 2 * 2:2], mixed[1:amount // 2 * 2:2]
    room = jnp.minimum(tallies[giver] - 1, bound - tallies[receiver]) // 2
    room = jnp.where((giver == sequence[0]) | (receiver == sequence[0]) | (tallies[receiver] == 0), 0, jnp.maximum(room, 0))
    shifted = jax.random.randint(jax.random.fold_in(own, 4), (amount // 2,), 0, 1 << 20) % (room + 1)
    tallies = tallies.at[giver].add(-shifted).at[receiver].add(shifted)
    items = jnp.searchsorted(jnp.cumsum(tallies), jnp.arange(rows * top), side="right").astype(jnp.int32)
    grid = items.reshape(top, rows).T
    grid = grid[jax.random.permutation(jax.random.fold_in(own, 1), rows)]
    offset_by = jax.random.randint(jax.random.fold_in(own, 2), (rows, 1), 0, top)
    return jnp.take_along_axis(grid, (jnp.arange(top)[None, :] + offset_by) % top, axis=1)


def portions_of(amount, total, bound, lean, full):
    loads = [(1 << 20) // math.isqrt(grade ** lean) + 1 for grade in range(1, amount + 1)]
    largest = bound if full else min(bound, max(-(-total // amount), total * loads[0] // sum(loads)))
    least = 1 if total - largest >= amount - 1 else 0
    holding, spare = [largest] + [least] * (amount - 1), total - largest - least * (amount - 1)
    while spare > 0:
        free = [i for i in range(1, amount) if holding[i] < largest] or [i for i in range(1, amount) if holding[i] < bound]
        pool, budget = sum([loads[i] for i in free]), spare
        for i in free:
            more = min(bound - holding[i], max(1, budget * loads[i] // pool), spare)
            holding[i] = holding[i] + more
            spare = spare - more
    return np.array(holding)


def centred(rng, shape, deviation, bound, pieces=(), kind=jnp.bfloat16):
    level = block_scale(rng, shape, pieces, -0.22, 0.18) if pieces else 1.0
    result = jax.random.normal(rng, shape, jnp.float32) * deviation * level
    return jnp.minimum(jnp.maximum(result, -bound), bound).astype(kind)


def setup_inputs(seed: int = 0, part: int = 0) -> dict:
    seeds = jax.random.split(jax.random.key(seed), 9)
    part_keys = jax.random.split(jax.random.fold_in(seeds[8], part), 9)
    replay = draw_replay(jax.random.fold_in(jax.random.fold_in(seeds[8], part), 71), part)
    sa_row = touch_ends(jax.random.randint(part_keys[1], (BATCH,), 0, REPLAY_DEV), jax.random.fold_in(part_keys[1], 1), 0, REPLAY_DEV - 1).astype(jnp.int32)
    goal_owner_keys = jax.random.split(jax.random.fold_in(part_keys[2], 1), BATCH // ROWS_DEV)
    goal_owner_turns = jax.random.permutation(jax.random.fold_in(part_keys[2], 3), BATCH // ROWS_DEV)
    goal_owner = jax.vmap(lambda own, number: routed_block(jax.random.fold_in(part_keys[2], 2), own, number, ROWS_DEV, N_DP, 1, CAP, 2))(goal_owner_keys, goal_owner_turns).reshape((BATCH, 1))
    goal_row = touch_ends(jax.random.randint(part_keys[3], (BATCH,), 0, REPLAY_DEV), jax.random.fold_in(part_keys[3], 1), 0, REPLAY_DEV - 1).astype(jnp.int32)
    state_first = centred(seeds[4], (LATENT, UNITS), LATENT ** -0.5, 0.1875, ((1, 4),))
    state_second = centred(seeds[5], (UNITS, EMBED), UNITS ** -0.5, 0.125, ((0, 4),))
    goal_first = centred(seeds[6], (LATENT, UNITS), LATENT ** -0.5, 0.1875, ((1, 4),))
    goal_second = centred(seeds[7], (UNITS, EMBED), UNITS ** -0.5, 0.125, ((0, 4),))
    return dict(replay=replay, sa_row=sa_row, goal_owner=goal_owner, goal_row=goal_row, state_first=state_first, state_second=state_second, goal_first=goal_first, goal_second=goal_second)


def silu_slope(value):
    sig = jax.nn.sigmoid(value)
    return sig * (1.0 + value * (1.0 - sig))

def encode(latent, first, second):
    pre = jnp.dot(latent, first, preferred_element_type=jnp.float32)
    act = jax.nn.silu(pre).astype(jnp.bfloat16)
    embed = jnp.dot(act, second, preferred_element_type=jnp.float32).astype(jnp.bfloat16)
    return (pre, act, embed)

def block_terms(latent, pre, act, grad, second):
    second_term = jnp.dot(act.T, grad, preferred_element_type=jnp.float32).astype(jnp.bfloat16)
    back = jnp.dot(grad, second.T, preferred_element_type=jnp.float32)
    slope = (back * silu_slope(pre)).astype(jnp.bfloat16)
    first_term = jnp.dot(latent.T, slope, preferred_element_type=jnp.float32).astype(jnp.bfloat16)
    return (first_term, second_term)

def reference(replay, sa_row, goal_owner, goal_row, state_first, state_second, goal_first, goal_second):
    block_of_row = jnp.arange(BATCH, dtype=jnp.int32) // ROWS_DEV
    state_x = jnp.take(replay, block_of_row * REPLAY_DEV + sa_row, axis=0)
    goal_x = jnp.take(replay, goal_owner[:, 0] * REPLAY_DEV + goal_row, axis=0)
    state_pre, state_act, phi = encode(state_x, state_first, state_second)
    goal_pre, goal_act, psi = encode(goal_x, goal_first, goal_second)
    scale = 4.0 / math.sqrt(EMBED)
    columns = jnp.arange(BATCH, dtype=jnp.int32)[None, :]

    def row_block(carry, inputs):
        index, phi_block = inputs
        scores = scale * jnp.dot(phi_block, psi.T, preferred_element_type=jnp.float32)
        top = lax.optimization_barrier(jnp.max(scores, axis=1, keepdims=True))
        lse = top + jnp.log(lax.optimization_barrier(jnp.sum(jnp.exp(scores - top), axis=1, keepdims=True)))
        row_ids = index * ROWS_DEV + jnp.arange(ROWS_DEV, dtype=jnp.int32)[:, None]
        weights = (jnp.exp(scores - lse) - (columns == row_ids).astype(jnp.float32)).astype(jnp.bfloat16)
        row_grad = (scale * jnp.dot(weights, psi, preferred_element_type=jnp.float32)).astype(jnp.bfloat16)
        term = (scale * jnp.dot(weights.T, phi_block, preferred_element_type=jnp.float32)).astype(jnp.bfloat16)
        term = lax.optimization_barrier(term)
        return (carry + term.astype(jnp.float32), row_grad)
    start = jnp.zeros((BATCH, EMBED), jnp.float32)
    blocks = (jnp.arange(N_DP, dtype=jnp.int32), phi.reshape(N_DP, ROWS_DEV, EMBED))
    column_total, phi_grad = lax.scan(row_block, start, blocks)
    phi_grad = phi_grad.reshape(BATCH, EMBED)
    psi_grad = column_total.astype(jnp.bfloat16)

    def shape_rows(array):
        return array.reshape((N_DP, ROWS_DEV) + array.shape[1:])

    def weight_block(carry, inputs):
        sx, spre, sact, sgrad, gx, gpre, gact, ggrad = inputs
        s_first, s_second = block_terms(sx, spre, sact, sgrad, state_second)
        g_first, g_second = block_terms(gx, gpre, gact, ggrad, goal_second)
        terms = (s_first, s_second, g_first, g_second)
        terms = lax.optimization_barrier(terms)
        return (tuple((c + t.astype(jnp.float32) for c, t in zip(carry, terms))), None)
    zeros_first = jnp.zeros((LATENT, UNITS), jnp.float32)
    zeros_second = jnp.zeros((UNITS, EMBED), jnp.float32)
    inputs = tuple((shape_rows(a) for a in (state_x, state_pre, state_act, phi_grad, goal_x, goal_pre, goal_act, psi_grad)))
    totals, unused = lax.scan(weight_block, (zeros_first, zeros_second, zeros_first, zeros_second), inputs)
    return (totals[0], totals[1], totals[2], totals[3])
```

```python
import functools
import math

import jax
import jax.numpy as jnp
from jax import lax
from jax.experimental import pallas as pl
from jax.experimental.pallas import tpu as pltpu
from jax.sharding import PartitionSpec as P


def silu_slope(value):
    sig = jax.nn.sigmoid(value)
    return sig * (1.0 + value * (1.0 - sig))


def slot_numbers(owner_list, shards):
    hits = (owner_list[:, None] == jnp.arange(shards, dtype=jnp.int32)[None, :]).astype(jnp.int32)
    before = jnp.cumsum(hits, axis=0) - hits
    return jnp.sum(before * hits, axis=1)


def local_terms(latent, pre, act, grad, second):
    second_term = jnp.einsum("ru,re->ue", act, grad, preferred_element_type=jnp.float32)
    back = jnp.einsum("re,ue->ru", grad, second, preferred_element_type=jnp.float32)
    slope = (back * silu_slope(pre)).astype(jnp.bfloat16)
    first_term = jnp.einsum("rl,ru->lu", latent, slope, preferred_element_type=jnp.float32)
    return (first_term, second_term)


def split_batch(replay, sa_row, goal_owner, goal_row, state_first, state_second, goal_first, goal_second):
    shards = lax.axis_size("dp")
    models = lax.axis_size("mp")
    here = lax.axis_index("dp")
    group = lax.axis_index("mp")
    rows = sa_row.shape[0]
    slots = 2 * rows // shards
    share = rows // models
    width = replay.shape[1]
    owners = goal_owner[:, 0]
    state_local = jnp.take(replay, sa_row, axis=0)
    position = owners * slots + slot_numbers(owners, shards)
    places = jnp.arange(shards * slots, dtype=jnp.int32)
    chosen = position[None, :] == places[:, None]
    requests = jnp.sum(jnp.where(chosen, goal_row[None, :], 0), axis=1).reshape(shards, slots)
    found = jnp.take(
        replay, lax.all_to_all(requests, "dp", split_axis=0, concat_axis=0, tiled=True), axis=0
    )
    returned = lax.all_to_all(found, "dp", split_axis=0, concat_axis=0, tiled=True)
    goal_local = jnp.take(returned.reshape(shards * slots, width), position, axis=0)
    state_x, goal_x = (
        lax.all_gather(state_local, "mp", axis=1, tiled=True),
        lax.all_gather(goal_local, "mp", axis=1, tiled=True),
    )
    state_pre = jnp.dot(state_x, state_first, preferred_element_type=jnp.float32)
    state_act = jax.nn.silu(state_pre).astype(jnp.bfloat16)
    state_part = jnp.dot(state_act, state_second, preferred_element_type=jnp.float32)
    goal_pre = jnp.dot(goal_x, goal_first, preferred_element_type=jnp.float32)
    goal_act = jax.nn.silu(goal_pre).astype(jnp.bfloat16)
    goal_part = jnp.dot(goal_act, goal_second, preferred_element_type=jnp.float32)
    state_total, goal_total = lax.psum((state_part, goal_part), "mp")
    phi = state_total.astype(jnp.bfloat16)
    psi_mine = lax.dynamic_slice_in_dim(goal_total, group * share, share, 0).astype(jnp.bfloat16)
    psi_cols = lax.all_gather(psi_mine, "dp", axis=0, tiled=True)
    scale = 4.0 / math.sqrt(phi.shape[1])
    scores = scale * jnp.einsum("re,ce->rc", phi, psi_cols, preferred_element_type=jnp.float32)
    local_top = jnp.max(scores, axis=1)
    top = lax.pmax(local_top, "mp")
    total = lax.psum(jnp.sum(jnp.exp(scores - top[:, None]), axis=1), "mp")
    lse = top + jnp.log(total)
    row_ids = jnp.arange(rows, dtype=jnp.int32)[:, None]
    col_ids = jnp.arange(scores.shape[1], dtype=jnp.int32)[None, :]
    target = here * share + row_ids - group * share
    positive = (row_ids // share == group) & (col_ids == target)
    weights = (jnp.exp(scores - lse[:, None]) - positive.astype(jnp.float32)).astype(jnp.bfloat16)
    row_part = scale * jnp.einsum(
        "rc,ce->re", weights, psi_cols, preferred_element_type=jnp.float32
    )
    phi_grad = lax.psum(row_part.astype(jnp.bfloat16), "mp")
    psi_grad_mine = lax.psum_scatter(
        (scale * jnp.einsum("rc,re->ce", weights, phi, preferred_element_type=jnp.float32)).astype(
            jnp.bfloat16
        ),
        "dp",
        scatter_dimension=0,
        tiled=True,
    )
    psi_grad = lax.all_gather(psi_grad_mine, "mp", axis=0, tiled=True)
    state_one, state_two = local_terms(state_x, state_pre, state_act, phi_grad, state_second)
    goal_one, goal_two = local_terms(goal_x, goal_pre, goal_act, psi_grad, goal_second)
    grads = (
        lax.psum_scatter(
            state_one.astype(jnp.bfloat16), "dp", scatter_dimension=0, tiled=True
        ).astype(jnp.float32),
        lax.psum_scatter(
            state_two.astype(jnp.bfloat16), "dp", scatter_dimension=1, tiled=True
        ).astype(jnp.float32),
        lax.psum_scatter(
            goal_one.astype(jnp.bfloat16), "dp", scatter_dimension=0, tiled=True
        ).astype(jnp.float32),
        lax.psum_scatter(
            goal_two.astype(jnp.bfloat16), "dp", scatter_dimension=1, tiled=True
        ).astype(jnp.float32),
    )
    return (grads[0], grads[1], grads[2], grads[3])


F32 = jnp.float32
BF16 = jnp.bfloat16


def call(kernel, outs, operands, scalars=0, scratch=(), limit=48, flops=0):
    smem = pl.BlockSpec(memory_space=pltpu.SMEM)
    vmem = pl.BlockSpec(memory_space=pltpu.VMEM)
    in_specs = [smem] * scalars + [vmem] * (len(operands) - scalars)
    moved = sum(a.size * a.dtype.itemsize for a in operands)
    moved += sum(math.prod(s) * jnp.dtype(d).itemsize for s, d in outs)
    return pl.pallas_call(
        kernel,
        out_shape=[jax.ShapeDtypeStruct(s, d) for s, d in outs],
        in_specs=in_specs,
        out_specs=[vmem] * len(outs),
        scratch_shapes=list(scratch),
        compiler_params=pltpu.CompilerParams(vmem_limit_bytes=limit * 2**20),
        cost_estimate=pl.CostEstimate(flops=flops, bytes_accessed=moved, transcendentals=0),
    )(*operands)


def dot(a, b, dims=((1,), (0,))):
    return lax.dot_general(a, b, (dims, ((), ())), preferred_element_type=F32)


def below(rows):
    earlier = lax.broadcasted_iota(jnp.int32, (rows, rows), 0)
    later = lax.broadcasted_iota(jnp.int32, (rows, rows), 1)
    return (earlier < later).astype(F32).astype(BF16)


def one_hot(column, width):
    lanes = lax.broadcasted_iota(jnp.int32, (column.shape[0], width), 1)
    return (column == lanes).astype(F32).astype(BF16)


def pick_kernel(row_ref, replay_ref, out_ref):
    rows = row_ref.shape[1]
    wide = jnp.broadcast_to(row_ref[...].astype(F32), (8, rows))
    column = wide.T[:, 0:1].astype(jnp.int32)
    out_ref[...] = dot(one_hot(column, replay_ref.shape[0]), replay_ref[...]).astype(BF16)


def found_kernel(shards, slots, here_ref, *refs):
    wants, replay_ref, out_ref, hits_ref = refs[:shards], refs[shards], refs[-2], refs[-1]
    here = here_ref[0]
    rows = wants[0].shape[1]
    hits_ref[...] = jnp.zeros_like(hits_ref)
    for step in range(shards):
        hits_ref[step : step + 1, :] = (wants[step][0:1, :] == here).astype(F32)
    before = dot(hits_ref[...].astype(BF16), below(rows))
    places = lax.broadcasted_iota(jnp.int32, (slots, rows), 0)
    for step in range(shards):
        rank = before[step : step + 1, :].astype(jnp.int32)
        chosen = (places == rank) & (wants[step][0:1, :] == here)
        asked = jnp.where(chosen, wants[step][1:2, :].astype(F32), 0.0)
        column = jnp.sum(asked, axis=1, keepdims=True).astype(jnp.int32)
        hot = one_hot(column, replay_ref.shape[0])
        out_ref[step * slots : (step + 1) * slots, :] = dot(hot, replay_ref[...]).astype(BF16)


def place_kernel(shards, slots, here_ref, *refs):
    wants, out_ref, place_ref = refs[:shards], refs[-2], refs[-1]
    here = here_ref[0]
    rows = wants[0].shape[1]
    tri = below(rows)
    place_ref[...] = jnp.zeros_like(place_ref)
    owners = lax.broadcasted_iota(jnp.int32, (place_ref.shape[0], rows), 0)
    for step in range(shards):
        owner = wants[step][0:1, :]
        hits = (owners == owner).astype(F32)
        rank = jnp.sum(dot(hits.astype(BF16), tri) * hits, axis=0, keepdims=True)
        turn = here - owner
        turn = jnp.where(turn < 0, turn + shards, turn)
        block = step - turn
        block = jnp.where(block < 0, block + shards, block)
        spot = ((turn * shards + block) * slots).astype(F32) + rank
        place_ref[step : step + 1, :] = spot
    out_ref[...] = place_ref[...].T


def select_kernel(shards, place_ref, *refs):
    founds, out_ref = refs[:shards], refs[-1]
    rows = place_ref.shape[0]
    size = founds[0].shape[0]
    for step in range(shards):
        column = place_ref[:, step : step + 1].astype(jnp.int32)
        total = dot(one_hot(column, size), founds[0][...])
        for turn in range(1, shards):
            total += dot(one_hot(column - turn * size, size), founds[turn][...])
        out_ref[step * rows : (step + 1) * rows, :] = total.astype(BF16)


def hidden(group, pieces, first_ref):
    width = pieces[0].shape[1]
    total = None
    for index, piece in enumerate(pieces):
        start = pl.multiple_of((group ^ index) * width, width)
        term = dot(piece[...], first_ref[pl.ds(start, width), :])
        total = term if total is None else total + term
    return total


def slope_of(value):
    sig = 1.0 / (1.0 + jnp.exp(-value))
    return sig * value, sig * (1.0 + value * (1.0 - sig))


def part_kernel(group_ref, *refs):
    pieces, (first_ref, second_ref, keep_ref, send_ref, part_ref) = refs[:4], refs[4:]
    group = group_ref[0]
    act, _ = slope_of(hidden(group, pieces, first_ref))
    part_ref[...] = dot(act.astype(BF16), second_ref[...])
    half = keep_ref.shape[0]
    core = group % 2
    keep_ref[...] = part_ref[pl.ds(pl.multiple_of(core * half, half), half), :]
    send_ref[...] = part_ref[pl.ds(pl.multiple_of((1 - core) * half, half), half), :]


def act_kernel(group_ref, *refs):
    pieces, (first_ref, act_ref, slope_ref) = refs[:-3], refs[-3:]
    act, slope = slope_of(hidden(group_ref[0], pieces, first_ref))
    act_ref[...] = act.astype(BF16)
    slope_ref[...] = slope


def embed_kernel(group_ref, *refs):
    pieces, firsts, seconds = refs[:4], refs[4:8], refs[8:12]
    psi_ref, act_ref, slope_ref, total_ref = refs[12:]
    group = group_ref[0]
    for index in range(4):
        act, slope = slope_of(hidden(group, pieces, firsts[index]))
        act = act.astype(BF16)
        if index == 0:
            act_ref[...] = act
            slope_ref[...] = slope
        term = dot(act, seconds[index][...])
        if index == 0:
            total_ref[...] = term
        elif index < 3:
            total_ref[...] += term
        else:
            psi_ref[...] = (total_ref[...] + term).astype(BF16)


def grads_kernel(shards, group_ref, here_ref, *refs):
    halves = refs[: 2 * shards]
    psi_ref, state_x, goal_x = refs[2 * shards], refs[2 * shards + 1 :][:4], refs[2 * shards + 5 :][:4]
    rest = refs[2 * shards + 9 :]
    state_act, state_slope, goal_act, goal_slope, state_second, goal_second = rest[:6]
    outs, (phi_ref, column_ref, grad_ref) = rest[6:10], rest[10:]
    group, here = group_ref[0], here_ref[0]
    half = halves[0].shape[0]
    core = group % 2
    for step in range(shards):
        for other in range(2):
            start = step * 2 * half + (core ^ other) * half
            phi_ref[pl.ds(pl.multiple_of(start, half), half), :] = halves[2 * step + other][...]
    batch, width = phi_ref.shape
    scale = 4.0 / math.sqrt(width)
    scores = scale * dot(phi_ref[...], psi_ref[...], ((1,), (1,)))
    top = jnp.max(scores, axis=1, keepdims=True)
    raised = jnp.exp(scores - top)
    share = raised * (1.0 / jnp.sum(raised, axis=1, keepdims=True))
    row_ids = lax.broadcasted_iota(jnp.int32, (batch, batch), 0)
    col_ids = lax.broadcasted_iota(jnp.int32, (batch, batch), 1)
    weights = (share - (row_ids == col_ids).astype(F32)).astype(BF16)
    columns = grad_ref.shape[1] // shards
    mine = pl.ds(pl.multiple_of(here * columns, columns), columns)
    sides = (
        (dot(weights, psi_ref[...]), state_x, state_act, state_slope, state_second, outs[:2]),
        (dot(weights, phi_ref[...], ((0,), (0,))), goal_x, goal_act, goal_slope, goal_second, outs[2:]),
    )
    for grad, pieces, act_ref, slope_ref, second_ref, (first_out, second_out) in sides:
        grad = (scale * grad).astype(BF16)
        grad_ref[...] = grad
        back = dot(grad, second_ref[...], ((1,), (1,)))
        slope = (back * slope_ref[...]).astype(BF16)
        for index in range(4):

            @pl.when((group ^ index) == here)
            def _(index=index):
                column_ref[...] = pieces[index][...]

        first_out[...] = dot(column_ref[...], slope, ((0,), (0,)))
        second_out[...] = dot(act_ref[...], grad_ref[:, mine], ((0,), (0,)))


def whole_batch(
    replay, sa_row, goal_owner, goal_row, state_first, state_second, goal_first, goal_second
):
    shards = lax.axis_size("dp")
    here = lax.axis_index("dp").astype(jnp.int32).reshape(1)
    group = lax.axis_index("mp").astype(jnp.int32).reshape(1)
    rows = sa_row.shape[0]
    slots = 2 * rows // shards
    width = replay.shape[1]
    units, embed = state_second.shape
    batch = shards * rows

    def around(array):
        turns = [[(i, (i + s) % shards) for i in range(shards)] for s in range(1, shards)]
        return [array] + [lax.ppermute(array, "dp", turn) for turn in turns]

    def swap(array, bit):
        return lax.ppermute(array, "mp", [(i, i ^ bit) for i in range(4)])

    want = jnp.concatenate([goal_owner.reshape(1, rows), goal_row.reshape(1, rows)], axis=0)
    wants = around(want)
    (state_mine,) = call(
        pick_kernel, [((rows, width), BF16)], [sa_row.reshape(1, rows), replay], flops=2 * rows * replay.size
    )
    state_near = [state_mine] + [swap(state_mine, bit) for bit in (1, 2, 3)]
    firsts = [goal_first, swap(goal_first, 1), swap(goal_first, 2)]
    seconds = [goal_second, swap(goal_second, 1), swap(goal_second, 2)]
    firsts.append(swap(firsts[2], 1))
    seconds.append(swap(seconds[2], 1))
    (found,) = call(
        functools.partial(found_kernel, shards, slots),
        [((shards * slots, width), BF16)],
        [here, *wants, replay],
        scalars=1,
        scratch=[pltpu.VMEM((8, rows), F32)],
        flops=2 * shards * slots * replay.size,
    )
    founds = around(found)
    (places,) = call(
        functools.partial(place_kernel, shards, slots),
        [((rows, 8), F32)],
        [here, *wants],
        scalars=1,
        scratch=[pltpu.VMEM((8, rows), F32)],
    )
    keep, send = call(
        part_kernel,
        [((rows // 2, embed), F32), ((rows // 2, embed), F32)],
        [group, *state_near, state_first, state_second],
        scalars=1,
        scratch=[pltpu.VMEM((rows, embed), F32)],
        flops=4 * rows * state_first.size,
    )
    chip = keep + swap(send, 1)
    phi_half = (chip + swap(chip, 2)).astype(BF16)
    phi_halves = []
    for piece in around(phi_half):
        phi_halves += [piece, swap(piece, 1)]
    state_all = jnp.concatenate(around(state_mine), axis=0)
    state_x = [state_all, swap(state_all, 1), swap(state_all, 2)]
    state_x.append(swap(state_x[2], 1))
    state_act, state_slope = call(
        act_kernel,
        [((batch, units), BF16), ((batch, units), F32)],
        [group, *state_x, state_first],
        scalars=1,
        flops=2 * batch * state_first.size,
    )
    (goal_all,) = call(
        functools.partial(select_kernel, shards),
        [((batch, width), BF16)],
        [places, *founds],
        flops=2 * batch * shards * found.size,
    )
    goal_x = [goal_all, swap(goal_all, 1), swap(goal_all, 2)]
    goal_x.append(swap(goal_x[2], 1))
    psi, goal_act, goal_slope = call(
        embed_kernel,
        [((batch, embed), BF16), ((batch, units), BF16), ((batch, units), F32)],
        [group, *goal_x, *firsts, *seconds],
        scalars=1,
        scratch=[pltpu.VMEM((batch, embed), F32)],
        flops=16 * batch * goal_first.size,
    )
    latents = 4 * width // shards
    outs = [((latents, units), F32), ((units, embed // shards), F32)]
    return tuple(
        call(
            functools.partial(grads_kernel, shards),
            outs + outs,
            [group, here, *phi_halves, psi, *state_x, *goal_x]
            + [state_act, state_slope, goal_act, goal_slope, state_second, goal_second],
            scalars=2,
            scratch=[
                pltpu.VMEM((batch, embed), BF16),
                pltpu.VMEM((batch, width), BF16),
                pltpu.VMEM((batch, embed), BF16),
            ],
            flops=6 * batch * batch * embed + 6 * batch * state_first.size,
        )
    )


def body(*args):
    shards, models = lax.axis_size("dp"), lax.axis_size("mp")
    rows = args[1].shape[0]
    if models == 4 and shards == 4 and shards * rows <= 1024:
        return whole_batch(*args)
    return split_batch(*args)


def solution(mesh):
    in_specs = (
        P(("groups", "dp"), "mp"),
        P(("groups", "dp")),
        P(("groups", "dp"), None),
        P(("groups", "dp")),
        P(None, "mp"),
        P("mp", None),
        P(None, "mp"),
        P("mp", None),
    )
    out_specs = (
        P(("groups", "dp"), "mp"),
        P(("groups", "mp"), "dp"),
        P(("groups", "dp"), "mp"),
        P(("groups", "mp"), "dp"),
    )
    return jax.shard_map(body, mesh=mesh, in_specs=in_specs, out_specs=out_specs, check_vma=False)
```

```python
import functools
import math

import jax
import jax.numpy as jnp
from jax import lax
from jax.experimental import pallas as pl
from jax.experimental.pallas import tpu as pltpu
from jax.sharding import PartitionSpec as P


def silu_slope(value):
    sig = jax.nn.sigmoid(value)
    return sig * (1.0 + value * (1.0 - sig))


def slot_numbers(owner_list, shards):
    hits = (owner_list[:, None] == jnp.arange(shards, dtype=jnp.int32)[None, :]).astype(jnp.int32)
    before = jnp.cumsum(hits, axis=0) - hits
    return jnp.sum(before * hits, axis=1)


def local_terms(latent, pre, act, grad, second):
    second_term = jnp.einsum("ru,re->ue", act, grad, preferred_element_type=jnp.float32)
    back = jnp.einsum("re,ue->ru", grad, second, preferred_element_type=jnp.float32)
    slope = (back * silu_slope(pre)).astype(jnp.bfloat16)
    first_term = jnp.einsum("rl,ru->lu", latent, slope, preferred_element_type=jnp.float32)
    return (first_term, second_term)


def split_batch(replay, sa_row, goal_owner, goal_row, state_first, state_second, goal_first, goal_second):
    shards = lax.axis_size("dp")
    models = lax.axis_size("mp")
    here = lax.axis_index("dp")
    group = lax.axis_index("mp")
    rows = sa_row.shape[0]
    slots = 2 * rows // shards
    share = rows // models
    width = replay.shape[1]
    owners = goal_owner[:, 0]
    state_local = jnp.take(replay, sa_row, axis=0)
    position = owners * slots + slot_numbers(owners, shards)
    places = jnp.arange(shards * slots, dtype=jnp.int32)
    chosen = position[None, :] == places[:, None]
    requests = jnp.sum(jnp.where(chosen, goal_row[None, :], 0), axis=1).reshape(shards, slots)
    found = jnp.take(
        replay, lax.all_to_all(requests, "dp", split_axis=0, concat_axis=0, tiled=True), axis=0
    )
    returned = lax.all_to_all(found, "dp", split_axis=0, concat_axis=0, tiled=True)
    goal_local = jnp.take(returned.reshape(shards * slots, width), position, axis=0)
    state_x, goal_x = (
        lax.all_gather(state_local, "mp", axis=1, tiled=True),
        lax.all_gather(goal_local, "mp", axis=1, tiled=True),
    )
    state_pre = jnp.dot(state_x, state_first, preferred_element_type=jnp.float32)
    state_act = jax.nn.silu(state_pre).astype(jnp.bfloat16)
    state_part = jnp.dot(state_act, state_second, preferred_element_type=jnp.float32)
    goal_pre = jnp.dot(goal_x, goal_first, preferred_element_type=jnp.float32)
    goal_act = jax.nn.silu(goal_pre).astype(jnp.bfloat16)
    goal_part = jnp.dot(goal_act, goal_second, preferred_element_type=jnp.float32)
    state_total, goal_total = lax.psum((state_part, goal_part), "mp")
    phi = state_total.astype(jnp.bfloat16)
    psi_mine = lax.dynamic_slice_in_dim(goal_total, group * share, share, 0).astype(jnp.bfloat16)
    psi_cols = lax.all_gather(psi_mine, "dp", axis=0, tiled=True)
    scale = 4.0 / math.sqrt(phi.shape[1])
    scores = scale * jnp.einsum("re,ce->rc", phi, psi_cols, preferred_element_type=jnp.float32)
    local_top = jnp.max(scores, axis=1)
    top = lax.pmax(local_top, "mp")
    total = lax.psum(jnp.sum(jnp.exp(scores - top[:, None]), axis=1), "mp")
    lse = top + jnp.log(total)
    row_ids = jnp.arange(rows, dtype=jnp.int32)[:, None]
    col_ids = jnp.arange(scores.shape[1], dtype=jnp.int32)[None, :]
    target = here * share + row_ids - group * share
    positive = (row_ids // share == group) & (col_ids == target)
    weights = (jnp.exp(scores - lse[:, None]) - positive.astype(jnp.float32)).astype(jnp.bfloat16)
    row_part = scale * jnp.einsum(
        "rc,ce->re", weights, psi_cols, preferred_element_type=jnp.float32
    )
    phi_grad = lax.psum(row_part.astype(jnp.bfloat16), "mp")
    psi_grad_mine = lax.psum_scatter(
        (scale * jnp.einsum("rc,re->ce", weights, phi, preferred_element_type=jnp.float32)).astype(
            jnp.bfloat16
        ),
        "dp",
        scatter_dimension=0,
        tiled=True,
    )
    psi_grad = lax.all_gather(psi_grad_mine, "mp", axis=0, tiled=True)
    state_one, state_two = local_terms(state_x, state_pre, state_act, phi_grad, state_second)
    goal_one, goal_two = local_terms(goal_x, goal_pre, goal_act, psi_grad, goal_second)
    grads = (
        lax.psum_scatter(
            state_one.astype(jnp.bfloat16), "dp", scatter_dimension=0, tiled=True
        ).astype(jnp.float32),
        lax.psum_scatter(
            state_two.astype(jnp.bfloat16), "dp", scatter_dimension=1, tiled=True
        ).astype(jnp.float32),
        lax.psum_scatter(
            goal_one.astype(jnp.bfloat16), "dp", scatter_dimension=0, tiled=True
        ).astype(jnp.float32),
        lax.psum_scatter(
            goal_two.astype(jnp.bfloat16), "dp", scatter_dimension=1, tiled=True
        ).astype(jnp.float32),
    )
    return (grads[0], grads[1], grads[2], grads[3])


F32 = jnp.float32
BF16 = jnp.bfloat16


def call(kernel, outs, operands, scalars=0, scratch=(), limit=32, flops=0):
    smem = pl.BlockSpec(memory_space=pltpu.SMEM)
    vmem = pl.BlockSpec(memory_space=pltpu.VMEM)
    in_specs = [smem] * scalars + [vmem] * (len(operands) - scalars)
    moved = sum(a.size * a.dtype.itemsize for a in operands)
    moved += sum(math.prod(s) * jnp.dtype(d).itemsize for s, d in outs)
    return pl.pallas_call(
        kernel,
        out_shape=[jax.ShapeDtypeStruct(s, d) for s, d in outs],
        in_specs=in_specs,
        out_specs=[vmem] * len(outs),
        scratch_shapes=list(scratch),
        compiler_params=pltpu.CompilerParams(vmem_limit_bytes=limit * 2**20),
        cost_estimate=pl.CostEstimate(flops=flops, bytes_accessed=moved, transcendentals=0),
    )(*operands)


def dot(a, b, dims=((1,), (0,))):
    return lax.dot_general(a, b, (dims, ((), ())), preferred_element_type=F32)


def below(rows):
    earlier = lax.broadcasted_iota(jnp.int32, (rows, rows), 0)
    later = lax.broadcasted_iota(jnp.int32, (rows, rows), 1)
    return (earlier < later).astype(F32).astype(BF16)


def one_hot(column, width):
    lanes = lax.broadcasted_iota(jnp.int32, (column.shape[0], width), 1)
    return (column == lanes).astype(F32).astype(BF16)


def pick_kernel(row_ref, owner_ref, goal_ref, replay_ref, out_ref, state_ref):
    rows = row_ref.shape[1]
    wide = jnp.broadcast_to(row_ref[...].astype(F32), (8, rows))
    column = wide.T[:, 0:1].astype(jnp.int32)
    picked = dot(one_hot(column, replay_ref.shape[0]), replay_ref[...]).astype(BF16)
    state_ref[...] = picked
    out_ref[0:rows, :] = picked
    shape = (out_ref.shape[0] - rows, rows)
    lines = lax.broadcasted_iota(jnp.int32, shape, 0)
    goal = goal_ref[...]
    code = jnp.where(lines == 0, owner_ref[...], jnp.where(lines == 1, goal >> 7, goal & 127))
    out_ref[rows:, :] = jnp.zeros((shape[0], out_ref.shape[1]), BF16)
    out_ref[rows:, 0:rows] = code.astype(F32).astype(BF16)


def found_kernel(shards, slots, here_ref, *refs):
    wants, replay_ref = refs[:shards], refs[shards]
    outs, all_ref, hits_ref = refs[shards + 1 : -2], refs[-2], refs[-1]
    here = here_ref[0]
    rows = hits_ref.shape[1]
    hits_ref[...] = jnp.zeros_like(hits_ref)
    codes = [want[rows:, 0:rows].astype(F32) for want in wants]
    owned = [code[0:1, :].astype(jnp.int32) == here for code in codes]
    for step in range(shards):
        hits_ref[step : step + 1, :] = owned[step].astype(F32)
    before = dot(hits_ref[...].astype(BF16), below(rows))
    places = lax.broadcasted_iota(jnp.int32, (slots, rows), 0)
    for step in range(shards):
        chosen = (places == before[step : step + 1, :].astype(jnp.int32)) & owned[step]
        goal = codes[step][1:2, :] * 128.0 + codes[step][2:3, :]
        column = jnp.sum(jnp.where(chosen, goal, 0.0), axis=1, keepdims=True).astype(jnp.int32)
        hot = one_hot(column, replay_ref.shape[0])
        outs[step][...] = dot(hot, replay_ref[...]).astype(BF16)
    for step in range(shards):
        all_ref[step * rows : (step + 1) * rows, :] = wants[step][0:rows, :]


def place_kernel(shards, slots, here_ref, owner_ref, out_ref):
    rows = owner_ref.shape[1]
    owner = owner_ref[...]
    hits = (lax.broadcasted_iota(jnp.int32, (8, rows), 0) == owner).astype(F32)
    rank = jnp.sum(dot(hits.astype(BF16), below(rows)) * hits, axis=0, keepdims=True)
    turn = owner - here_ref[0]
    turn = jnp.where(turn < 0, turn + shards, turn)
    spot = (turn * slots).astype(F32) + rank
    column = jnp.broadcast_to(spot, (8, rows)).T[:, 0:1].astype(jnp.int32)
    out_ref[...] = one_hot(column, shards * slots)


def select_kernel(hot_ref, *refs):
    founds, out_ref, held_ref = refs[:-2], refs[-2], refs[-1]
    slots = founds[0].shape[0]
    for turn, found in enumerate(founds):
        held_ref[turn * slots : (turn + 1) * slots, :] = found[...]
    out_ref[...] = dot(hot_ref[...], held_ref[...]).astype(BF16)


def hidden(group, pieces, first_ref):
    width = pieces[0].shape[1]
    total = None
    for index, piece in enumerate(pieces):
        start = pl.multiple_of((group ^ index) * width, width)
        term = dot(piece[...], first_ref[pl.ds(start, width), :])
        total = term if total is None else total + term
    return total


def slope_of(value):
    sig = 1.0 / (1.0 + jnp.exp(-value))
    return sig * value, sig * (1.0 + value * (1.0 - sig))


def part_kernel(group_ref, *refs):
    pieces, (first_ref, second_ref, keep_ref, send_ref, part_ref) = refs[:4], refs[4:]
    group = group_ref[0]
    act, _ = slope_of(hidden(group, pieces, first_ref))
    part_ref[...] = dot(act.astype(BF16), second_ref[...])
    half = keep_ref.shape[0]
    core = group % 2
    keep_ref[...] = part_ref[pl.ds(pl.multiple_of(core * half, half), half), :]
    send_ref[...] = part_ref[pl.ds(pl.multiple_of((1 - core) * half, half), half), :]


def act_kernel(group_ref, *refs):
    pieces, (first_ref, act_ref, slope_ref) = refs[:-3], refs[-3:]
    act, slope = slope_of(hidden(group_ref[0], pieces, first_ref))
    act_ref[...] = act.astype(BF16)
    slope_ref[...] = slope


def grads_kernel(shards, group_ref, here_ref, *refs):
    halves, refs = (refs[: 2 * shards], refs[2 * shards : 4 * shards]), refs[4 * shards :]
    state_x, goal_x, refs = refs[:4], refs[4:8], refs[8:]
    state_act, state_slope, goal_act, goal_slope, state_second, goal_second = refs[:6]
    outs, (phi_ref, psi_ref, column_ref, grad_ref) = refs[6:10], refs[10:]
    group, here = group_ref[0], here_ref[0]
    half = halves[0][0].shape[0]
    core = group % 2
    for pieces, whole_ref in zip(halves, (phi_ref, psi_ref)):
        for step in range(shards):
            for other in range(2):
                start = step * 2 * half + (core ^ other) * half
                whole_ref[pl.ds(pl.multiple_of(start, half), half), :] = pieces[2 * step + other][...]
    batch, width = phi_ref.shape
    scale = 4.0 / math.sqrt(width)
    scores = scale * dot(phi_ref[...], psi_ref[...], ((1,), (1,)))
    top = jnp.max(scores, axis=1, keepdims=True)
    raised = jnp.exp(scores - top)
    share = raised * (1.0 / jnp.sum(raised, axis=1, keepdims=True))
    row_ids = lax.broadcasted_iota(jnp.int32, (batch, batch), 0)
    col_ids = lax.broadcasted_iota(jnp.int32, (batch, batch), 1)
    weights = (share - (row_ids == col_ids).astype(F32)).astype(BF16)
    columns = grad_ref.shape[1] // shards
    mine = pl.ds(pl.multiple_of(here * columns, columns), columns)
    sides = (
        (dot(weights, psi_ref[...]), state_x, state_act, state_slope, state_second, outs[:2]),
        (dot(weights, phi_ref[...], ((0,), (0,))), goal_x, goal_act, goal_slope, goal_second, outs[2:]),
    )
    for grad, pieces, act_ref, slope_ref, second_ref, (first_out, second_out) in sides:
        grad = (scale * grad).astype(BF16)
        grad_ref[...] = grad
        back = dot(grad, second_ref[...], ((1,), (1,)))
        slope = (back * slope_ref[...]).astype(BF16)
        for index in range(4):

            @pl.when((group ^ index) == here)
            def _(index=index):
                column_ref[...] = pieces[index][...]

        first_out[...] = dot(column_ref[...], slope, ((0,), (0,)))
        second_out[...] = dot(act_ref[...], grad_ref[:, mine], ((0,), (0,)))


def whole_batch(
    replay, sa_row, goal_owner, goal_row, state_first, state_second, goal_first, goal_second
):
    shards = lax.axis_size("dp")
    here = lax.axis_index("dp").astype(jnp.int32).reshape(1)
    group = lax.axis_index("mp").astype(jnp.int32).reshape(1)
    rows = sa_row.shape[0]
    slots = 2 * rows // shards
    width = replay.shape[1]
    units, embed = state_second.shape
    batch = shards * rows

    def turn(array, step):
        return lax.ppermute(array, "dp", [(i, (i + step) % shards) for i in range(shards)])

    def around(array):
        return [array] + [turn(array, step) for step in range(1, shards)]

    def swap(array, bit):
        return lax.ppermute(array, "mp", [(i, i ^ bit) for i in range(4)])

    def near(array):
        return [array] + [swap(array, bit) for bit in (1, 2, 3)]

    def chip_wide(array):
        across = swap(array, 2)
        return [array, swap(array, 1), across, swap(across, 1)]

    def embed_rows(pieces, first, second):
        keep, send = call(
            part_kernel,
            [((rows // 2, embed), F32), ((rows // 2, embed), F32)],
            [group, *pieces, first, second],
            scalars=1,
            scratch=[pltpu.VMEM((rows, embed), F32)],
            flops=4 * rows * first.size,
        )
        chip = keep + swap(send, 1)
        half = (chip + swap(chip, 2)).astype(BF16)
        halves = []
        for piece in around(half):
            halves += [piece, swap(piece, 1)]
        return halves

    def hidden_rows(pieces, first):
        return call(
            act_kernel,
            [((batch, units), BF16), ((batch, units), F32)],
            [group, *pieces, first],
            scalars=1,
            flops=2 * batch * first.size,
        )

    owner = goal_owner.reshape(1, rows)
    carried, state_mine = call(
        pick_kernel,
        [((rows + 16, width), BF16), ((rows, width), BF16)],
        [sa_row.reshape(1, rows), owner, goal_row.reshape(1, rows), replay],
        flops=2 * rows * replay.size,
    )
    wants = around(carried)
    state_near = near(state_mine)
    *founds, state_all = call(
        functools.partial(found_kernel, shards, slots),
        [((slots, width), BF16)] * shards + [((batch, width), BF16)],
        [here, *wants, replay],
        scalars=1,
        scratch=[pltpu.VMEM((8, rows), F32)],
        flops=2 * shards * slots * replay.size,
    )
    founds = [founds[0]] + [turn(founds[step], shards - step) for step in range(1, shards)]
    (hot,) = call(
        functools.partial(place_kernel, shards, slots),
        [((rows, shards * slots), BF16)],
        [here, owner],
        scalars=1,
    )
    phi = embed_rows(state_near, state_first, state_second)
    (goal_mine,) = call(
        select_kernel,
        [((rows, width), BF16)],
        [hot, *founds],
        scratch=[pltpu.VMEM((shards * slots, width), BF16)],
    )
    psi = embed_rows(near(goal_mine), goal_first, goal_second)
    goal_all = jnp.concatenate(around(goal_mine), axis=0)
    state_x = chip_wide(state_all)
    goal_x = chip_wide(goal_all)
    state_act, state_slope = hidden_rows(state_x, state_first)
    goal_act, goal_slope = hidden_rows(goal_x, goal_first)
    latents = 4 * width // shards
    outs = [((latents, units), F32), ((units, embed // shards), F32)]
    return tuple(
        call(
            functools.partial(grads_kernel, shards),
            outs + outs,
            [group, here, *phi, *psi, *state_x, *goal_x]
            + [state_act, state_slope, goal_act, goal_slope, state_second, goal_second],
            scalars=2,
            scratch=[
                pltpu.VMEM((batch, embed), BF16),
                pltpu.VMEM((batch, embed), BF16),
                pltpu.VMEM((batch, width), BF16),
                pltpu.VMEM((batch, embed), BF16),
            ],
            flops=6 * batch * batch * embed + 6 * batch * state_first.size,
        )
    )


def body(*args):
    shards, models = lax.axis_size("dp"), lax.axis_size("mp")
    rows = args[1].shape[0]
    if models == 4 and shards == 4 and shards * rows <= 1024:
        return whole_batch(*args)
    return split_batch(*args)


def solution(mesh):
    in_specs = (
        P(("groups", "dp"), "mp"),
        P(("groups", "dp")),
        P(("groups", "dp"), None),
        P(("groups", "dp")),
        P(None, "mp"),
        P("mp", None),
        P(None, "mp"),
        P("mp", None),
    )
    out_specs = (
        P(("groups", "dp"), "mp"),
        P(("groups", "mp"), "dp"),
        P(("groups", "dp"), "mp"),
        P(("groups", "mp"), "dp"),
    )
    return jax.shard_map(body, mesh=mesh, in_specs=in_specs, out_specs=out_specs, check_vma=False)
```
